128 devices in a mesh: fsdp: 16 (over x, y_hi, core), user: 8 (over y_lo, z).
Axes of the slice: x: 4, y: 4 (y_hi: 2, y_lo: 2; y = y_hi * 2 + y_lo), z: 4, core: 2. Of those that a mesh axis runs over, the one named last changes fastest.
Arguments:
- gate_pre: bfloat16 [16384, 18432], P('fsdp', 'user'), may hold values from -6 to 6
- up_pre: bfloat16 [16384, 18432], P('fsdp', 'user'), may hold values from -6 to 6
- out_grad: bfloat16 [16384, 2304], P(('fsdp', 'user')), may hold values from -16 to 16
- down_weight: bfloat16 [18432, 2304], P('user', 'fsdp'), may hold values from -0.046875 to 0.046875
- token_user: int32 [16384, 1], P('fsdp'), may hold values from 0 to 15, as said below
- noise: float32 [18432, 2304], P('user', 'fsdp'), may hold values from -1.5 to 1.5
Outputs:
- gate_grad: bfloat16 [16384, 18432], P('fsdp', 'user')
- up_grad: bfloat16 [16384, 18432], P('fsdp', 'user')
- weight_update: float32 [18432, 2304], P('user', 'fsdp')
The draws below stay inside these ranges and needn't reach their ends.
Inputs may be any that keep to these rules, and one draw needn't show every extreme that they name: `token_user`: within the rows of one group (1024 rows, one index of fsdp) no user is named by more than 128 rows, and some user by exactly 128.
All inputs are finite; a program needn't handle non-finite values.
Results may differ from the reference program's by a relative error of at most 0.01.
Values may be sent and summed in bfloat16 or wider, within the bound.
No kernel may reach another device: no remote copies, remote signals or barrier semaphores. Data moves between devices by JAX's collectives and lax.ppermute only.
A program may use at most 256 MiB of HBM per device.

```python
import math
import jax
import jax.numpy as jnp
from jax import lax

D = 2304
F = 18432
TOK_DEV = 128
SLOTS = 128
USR_DEV = 2
GROUP_TOK = 1024
USERS_GRP = 16
TOKENS = 16384
USERS = 256
N_FSDP = 16
N_USER = 8


shared_weight = 0.9


own_weight = math.sqrt(1.0 - 0.81)


cluster_count = 4


def user_plan(key):
    group_count = TOKENS // GROUP_TOK
    slot_total = USERS_GRP * SLOTS
    positions = jnp.arange(slot_total, dtype=jnp.int32)
    slot_user = positions // SLOTS
    slot_rank = positions % SLOTS
    key_steps = jax.random.fold_in(key, 101)
    key_jitter = jax.random.fold_in(key, 102)
    key_full = jax.random.fold_in(key, 103)
    key_shuffle = jax.random.fold_in(key, 104)
    key_cluster = jax.random.fold_in(key, 105)
    key_signs = jax.random.fold_in(key, 106)
    user_steps = jax.random.randint(key_steps, (group_count, USERS_GRP), 0, 4096, dtype=jnp.int32)
    slot_step = jnp.take(user_steps, slot_user, axis=1)
    jitter = jax.random.randint(key_jitter, (group_count, slot_total), 0, 262144, dtype=jnp.int32)
    full_user = jax.random.randint(key_full, (group_count, 1), 0, USERS_GRP, dtype=jnp.int32)
    scores = jitter - slot_rank[None, :] * slot_step
    scores = scores + jnp.where(slot_user[None, :] == full_user, 8388608, 0).astype(jnp.int32)
    scores = scores + jnp.where(slot_rank[None, :] == 0, 4194304, 0).astype(jnp.int32)
    ranking = jnp.argsort(-scores, axis=1, stable=True)
    chosen = ranking[:, :GROUP_TOK] // SLOTS
    shuffle_keys = jax.random.randint(key_shuffle, (group_count, GROUP_TOK), 0, 1073741824, dtype=jnp.int32)
    shuffle = jnp.argsort(shuffle_keys, axis=1, stable=True)
    token_users = jnp.take_along_axis(chosen, shuffle, axis=1).astype(jnp.int32)
    cluster = jax.random.randint(key_cluster, (group_count, GROUP_TOK), 0, cluster_count, dtype=jnp.int32)
    sign_bits = jax.random.randint(key_signs, (group_count, GROUP_TOK), 0, 2, dtype=jnp.int32)
    group_index = jnp.arange(group_count, dtype=jnp.int32)[:, None]
    table_row = (group_index * USERS_GRP + token_users) * cluster_count + cluster
    sign_value = (2 * sign_bits - 1).astype(jnp.float32)
    return (token_users.reshape(TOKENS), table_row.reshape(TOKENS), sign_value.reshape(TOKENS))


def draw_token_user(key, part):
    token_users, table_row, sign_value = user_plan(key)
    return token_users.reshape(TOKENS, 1)


def draw_up_pre(key, part):
    token_users, table_row, sign_value = user_plan(key)
    key = jax.random.fold_in(key, 5)
    key_table = jax.random.fold_in(key, 1)
    key_own = jax.random.fold_in(key, 2)
    comp_table = jax.random.normal(key_table, (USERS * cluster_count, F), jnp.float32)
    own_part = jax.random.normal(key_own, (TOKENS, F), jnp.float32)
    shared_part = jnp.take(comp_table, table_row, axis=0) * sign_value[:, None]
    result_value = own_weight * own_part + shared_weight * shared_part
    return jnp.clip(result_value, -6.0, 6.0).astype(jnp.bfloat16)


def draw_out_grad(key, part):
    token_users, table_row, sign_value = user_plan(key)
    key = jax.random.fold_in(key, 7)
    key_table = jax.random.fold_in(key, 1)
    key_own = jax.random.fold_in(key, 2)
    key_pairing = jax.random.fold_in(key, 3)
    group_count = TOKENS // GROUP_TOK
    comp_table = jax.random.normal(key_table, (USERS * cluster_count, D), jnp.float32)
    own_part = jax.random.normal(key_own, (TOKENS, D), jnp.float32)
    shared_part = jnp.take(comp_table, table_row, axis=0) * sign_value[:, None]
    pairing = jax.random.permutation(key_pairing, group_count)
    col_width = D // group_count
    col_block = jnp.arange(D, dtype=jnp.int32) // col_width
    row_group = jnp.arange(TOKENS, dtype=jnp.int32) // GROUP_TOK
    target_block = jnp.take(pairing, row_group, axis=0)
    spike_gain = jnp.where(col_block[None, :] == target_block[:, None], 3.0, 1.0).astype(jnp.float32)
    result_value = (own_weight * own_part + shared_weight * shared_part) * spike_gain
    return jnp.clip(result_value, -16.0, 16.0).astype(jnp.bfloat16)


def levels(key, extent, shards, smallest, largest):
    level = 1.0
    for dim, blocks in shards:
        heights = jax.random.uniform(jax.random.fold_in(jax.random.fold_in(key, 6), dim), (blocks,), jnp.float32, smallest / len(shards), largest / len(shards))
        level = level * jnp.repeat(jnp.exp(heights), extent[dim] // blocks).reshape((-1,) + (1,) * (len(extent) - 1 - dim))
    return level


def normal_values(key, shape, width, reach, cuts=(), held_as=jnp.bfloat16):
    level = levels(key, shape, cuts, -0.22, 0.18) if cuts else 1.0
    result = jax.random.normal(key, shape, jnp.float32) * width * level
    return jnp.minimum(jnp.maximum(result, -reach), reach).astype(held_as)


def setup_inputs(seed: int = 0) -> dict:
    key_list = jax.random.split(jax.random.key(seed), 7)
    return {
        "gate_pre": normal_values(key_list[0], (TOKENS, F), 1.0, 6.0, ((0, 16), (1, 8))),
        "up_pre": draw_up_pre(jax.random.fold_in(key_list[6], 71), 0),
        "out_grad": draw_out_grad(jax.random.fold_in(key_list[6], 71), 0),
        "down_weight": normal_values(key_list[3], (F, D), F ** -0.5, 0.046875, ((0, 8), (1, 16))),
        "token_user": draw_token_user(jax.random.fold_in(key_list[6], 71), 0),
        "noise": normal_values(key_list[5], (F, D), 0.1, 1.5, ((0, 8), (1, 16)), jnp.float32),
    }


root_two_pi = math.sqrt(2.0 / math.pi)

def gelu_parts(gate):
    inner_term = gate + 0.044715 * gate * gate * gate
    tanh_value = jnp.tanh(root_two_pi * inner_term)
    gelu_value = 0.5 * gate * (1.0 + tanh_value)
    gelu_slope = 0.5 * (1.0 + tanh_value) + 0.5 * gate * (1.0 - tanh_value * tanh_value) * root_two_pi * (1.0 + 3.0 * 0.044715 * gate * gate)
    return (gelu_value, gelu_slope)

def reference(gate_pre, up_pre, out_grad, down_weight, token_user, noise):
    group_tok = TOK_DEV * N_USER
    users_group = USR_DEV * N_USER
    clip_bound = 0.5 * math.sqrt(SLOTS * F * D)
    gates = gate_pre.reshape(N_FSDP, group_tok, F)
    uppers = up_pre.reshape(N_FSDP, group_tok, F)
    grads = out_grad.reshape(N_FSDP, group_tok, D)
    owners = token_user[:, 0].reshape(N_FSDP, group_tok)

    def one_group(total, pieces):
        gate_g, up_g, grad_g, user_g = pieces
        gate_f = gate_g.astype(jnp.float32)
        up_f = up_g.astype(jnp.float32)
        gelu_value, gelu_slope = gelu_parts(gate_f)
        hidden = (gelu_value * up_f).astype(jnp.bfloat16)
        hidden_grad = jnp.dot(grad_g, down_weight.T, preferred_element_type=jnp.float32)
        gate_out = (hidden_grad * up_f * gelu_slope).astype(jnp.bfloat16)
        up_out = (hidden_grad * gelu_value).astype(jnp.bfloat16)
        hidden_gram = jnp.dot(hidden, hidden.T, preferred_element_type=jnp.float32)
        grad_gram = jnp.dot(grad_g, grad_g.T, preferred_element_type=jnp.float32)
        same = user_g[:, None] == user_g[None, :]
        row_terms = lax.optimization_barrier(jnp.sum(jnp.where(same, hidden_gram * grad_gram, 0.0), axis=1))
        onehot = (user_g[:, None] == jnp.arange(users_group, dtype=jnp.int32)[None, :]).astype(jnp.float32)
        squares = lax.optimization_barrier(jnp.sum(onehot * row_terms[:, None], axis=0))
        factor = clip_bound / jnp.maximum(jnp.sqrt(squares), clip_bound)
        row_factor = lax.optimization_barrier(jnp.sum(onehot * factor[None, :], axis=1))
        scaled = (grad_g.astype(jnp.float32) * row_factor[:, None]).astype(jnp.bfloat16)
        group_term = jnp.dot(hidden.T, scaled, preferred_element_type=jnp.float32).astype(jnp.bfloat16)
        total = total + group_term.astype(jnp.float32)
        return (total, (gate_out, up_out))
    total, outs = lax.scan(one_group, jnp.zeros((F, D), jnp.float32), (gates, uppers, grads, owners))
    gate_grad = outs[0].reshape(TOKENS, F)
    up_grad = outs[1].reshape(TOKENS, F)
    scale = math.sqrt(F * D) / (USERS * clip_bound)
    return (gate_grad, up_grad, scale * total + noise)
```

```python
import functools
import math

import jax
import jax.numpy as jnp
from jax import lax
from jax.experimental import pallas as pl
from jax.experimental.pallas import tpu as pltpu
from jax.sharding import Mesh, PartitionSpec as P

D = 2304
F = 18432
SLOTS = 128
USR_DEV = 2
NX, NY, NC, NP, NZ = 4, 2, 2, 2, 4
TILE = 256
MIB = 2**20

root_two_pi = math.sqrt(2.0 / math.pi)
VMEM = pl.BlockSpec(memory_space=pltpu.VMEM)
SMEM = pl.BlockSpec(memory_space=pltpu.SMEM)
ANY = pl.BlockSpec(memory_space=pl.ANY)


def gelu_parts(gate):
    square = gate * gate
    tanh_value = jnp.tanh(gate * (root_two_pi + (root_two_pi * 0.044715) * square))
    share = 0.5 + 0.5 * tanh_value
    gelu_slope = share + (0.5 * gate) * (1.0 - tanh_value * tanh_value) * (
        root_two_pi + (root_two_pi * 3.0 * 0.044715) * square
    )
    return (gate * share, gelu_slope)


def shift(count, by):
    return [(i, (i + by) % count) for i in range(count)]


LITTLE = pl.CostEstimate(flops=1, bytes_accessed=1, transcendentals=0)
TOKEN = jax.ShapeDtypeStruct((8, 128), jnp.float32)


def params(mib, *semantics):
    return pltpu.CompilerParams(
        vmem_limit_bytes=mib * MIB, dimension_semantics=semantics or None
    )


def hidden_kernel(gate_ref, up_ref, hidden_ref):
    gelu_value, _ = gelu_parts(gate_ref[...].astype(jnp.float32))
    hidden_ref[...] = (gelu_value * up_ref[...].astype(jnp.float32)).astype(jnp.bfloat16)


def hidden_call(gate, up):
    rows, cols = gate.shape
    spec = pl.BlockSpec((TILE // 2, cols), lambda i: (i, 0))
    return pl.pallas_call(
        hidden_kernel,
        grid=(2 * rows // TILE,),
        in_specs=[spec, spec],
        out_specs=spec,
        out_shape=jax.ShapeDtypeStruct(gate.shape, jnp.bfloat16),
        compiler_params=params(40, "arbitrary"),
        cost_estimate=LITTLE,
        name="hidden",
    )(gate, up)


def tiles_of(rows):
    count = rows // TILE
    return [(i, j) for i in range(count) for j in range(i, count)]


def outer(left, right):
    return lax.dot_general(
        left, right, (((1,), (1,)), ((), ())), preferred_element_type=jnp.float32
    )


def hidden_gram_kernel(hidden_ref, user_ref, user_row_ref, gram_ref):
    for k, (i, j) in enumerate(tiles_of(hidden_ref.shape[0])):
        first, second = pl.ds(i * TILE, TILE), pl.ds(j * TILE, TILE)
        tile = outer(hidden_ref[first, :], hidden_ref[second, :])
        same = user_ref[first, :] == user_row_ref[:, second]
        gram_ref[k] = jnp.where(same, tile if i == j else 2.0 * tile, 0.0)


def hidden_gram_call(hidden, user, user_row):
    rows, cols = hidden.shape
    count = len(tiles_of(rows))
    return pl.pallas_call(
        hidden_gram_kernel,
        in_specs=[VMEM, VMEM, VMEM],
        out_specs=VMEM,
        out_shape=jax.ShapeDtypeStruct((count, TILE, TILE), jnp.float32),
        compiler_params=params(24),
        cost_estimate=LITTLE,
        name="hidden_gram",
    )(hidden, user, user_row)


def grad_gram_kernel(place_ref, *refs):
    count = len(refs) - 5
    pieces = refs[:count]
    gram_ref, user_row_ref, grad_ref, squares_ref, sems = refs[count:]
    copies = []
    for k, piece in enumerate(pieces):
        size = piece.shape[0]
        start = pl.multiple_of(place_ref[k + 3], size)
        copies.append(pltpu.make_async_copy(piece, grad_ref.at[pl.ds(start, size)], sems.at[k]))
    for copy in copies:
        copy.start()
    for copy in copies:
        copy.wait()
    rows = grad_ref.shape[0]
    terms = [None] * (rows // TILE)
    for k, (i, j) in enumerate(tiles_of(rows)):
        tile = outer(grad_ref[pl.ds(i * TILE, TILE), :], grad_ref[pl.ds(j * TILE, TILE), :])
        term = jnp.sum(tile * gram_ref[k], axis=0, keepdims=True)
        terms[j] = term if terms[j] is None else terms[j] + term
    terms = jnp.concatenate(terms, axis=1)
    users = lax.broadcasted_iota(jnp.int32, (squares_ref.shape[0], rows), 0)
    chosen = jnp.where(users == user_row_ref[...], terms, 0.0)
    squares_ref[...] = jnp.broadcast_to(
        jnp.sum(chosen, axis=1, keepdims=True), squares_ref.shape
    )


def grad_gram_call(place, pieces, gram, user_row, users_group):
    rows, cols = user_row.shape[1], pieces[0].shape[1]
    return pl.pallas_call(
        grad_gram_kernel,
        in_specs=[SMEM] + [ANY] * len(pieces) + [VMEM] * 2,
        out_specs=[VMEM] * 2,
        out_shape=[
            jax.ShapeDtypeStruct((rows, cols), jnp.bfloat16),
            jax.ShapeDtypeStruct((users_group, 128), jnp.float32),
        ],
        scratch_shapes=[pltpu.SemaphoreType.DMA((len(pieces),))],
        compiler_params=params(40),
        cost_estimate=LITTLE,
        name="grad_gram",
    )(place, *pieces, gram, user_row)


def transpose_kernel(place_ref, grad_ref, mine_ref, other_ref):
    core = place_ref[0]
    count, width, _ = mine_ref.shape
    turned = grad_ref[...].T
    for k in range(count):
        first, second = (turned[(2 * k + i) * width : (2 * k + i + 1) * width] for i in range(2))
        mine_ref[k] = jnp.where(core == 0, first, second)
        other_ref[k] = jnp.where(core == 0, second, first)


def transpose_call(place, grad, width):
    rows, cols = grad.shape
    count = cols // width // NC
    out = pl.BlockSpec((count // 2, width, rows), lambda i: (i, 0, 0))
    return pl.pallas_call(
        transpose_kernel,
        grid=(2,),
        in_specs=[SMEM, pl.BlockSpec((rows, cols // 2), lambda i: (0, i))],
        out_specs=[out, out],
        out_shape=[jax.ShapeDtypeStruct((count, width, rows), grad.dtype)] * 2,
        compiler_params=params(40, "arbitrary"),
        cost_estimate=LITTLE,
        name="transpose",
    )(place, grad)


def scale_rows(
    clip_bound, place_ref, mine_ref, theirs_ref, squares_ref, more_ref, user_refs, scaled_ref
):
    width, rows = mine_ref.shape[1:]
    count = squares_ref.shape[0] // 2
    ids = lax.broadcasted_iota(jnp.int32, (count, rows), 0)
    x_index, y_index = place_ref[1], place_ref[2]
    for group, ref in enumerate((mine_ref, theirs_ref)):
        inside = pl.ds(group * count, count)
        squares = squares_ref[inside, 0:1] + more_ref[inside, 0:1]
        factor = clip_bound / jnp.maximum(jnp.sqrt(squares), clip_bound)
        chosen = jnp.where(ids == user_refs[group][...], factor, 0.0)
        row_factor = jnp.sum(chosen, axis=0, keepdims=True)
        for dx in range(NX):
            for dy in range(NY):
                block = ref[((x_index + dx) % NX) * NY + (y_index + dy) % NY]
                scaled_ref[
                    pl.ds((dx * NY + dy) * width, width), pl.ds(group * rows, rows)
                ] = (block.astype(jnp.float32) * row_factor).astype(jnp.bfloat16)


def term_kernel(
    clip_bound, by_x, place_ref, mine_ref, theirs_ref, own_ref, sib_ref, squares_ref, more_ref,
    user_ref, user_sib_ref, after_ref, *refs
):
    outs, token_ref, scaled_ref = refs[:-2], refs[-2], refs[-1]
    token_ref[...] = jnp.zeros_like(token_ref)

    @pl.when(pl.program_id(0) == 0)
    def _():
        scale_rows(
            clip_bound, place_ref, mine_ref, theirs_ref, squares_ref, more_ref,
            (user_ref, user_sib_ref), scaled_ref,
        )

    rows = own_ref.shape[0]
    total = jnp.dot(scaled_ref[:, :rows], own_ref[...], preferred_element_type=jnp.float32)
    total += jnp.dot(scaled_ref[:, rows:], sib_ref[...], preferred_element_type=jnp.float32)
    total = total.astype(jnp.bfloat16)
    size = mine_ref.shape[1]
    for dx in range(NX):
        for dy in range(NY):
            out, at = (outs[dx], dy) if by_x else (outs[2 * dy + dx // 2], dx % 2)
            out[pl.ds(at * size, size), :] = total[(dx * NY + dy) * size :][:size]


def term_call(
    by_x, place, mine, theirs, own, sib, squares, more, user_row, user_sib, clip_bound, start, cols,
    after
):
    count, width, rows = mine.shape
    whole = lambda a: pl.BlockSpec(a.shape, lambda n: (0,) * a.ndim)
    hidden = pl.BlockSpec((rows, TILE), lambda n: (0, n + start // TILE))
    pieces = NX if by_x else 2 * NY
    size = count * width // pieces
    small = [squares, more, user_row, user_sib]
    return pl.pallas_call(
        functools.partial(term_kernel, clip_bound, by_x),
        grid=(cols // TILE,),
        in_specs=[SMEM, whole(mine), whole(theirs), hidden, hidden] + [whole(a) for a in small] + [ANY],
        out_specs=[pl.BlockSpec((size, TILE), lambda n: (0, n))] * pieces + [whole(TOKEN)],
        out_shape=[jax.ShapeDtypeStruct((size, cols), jnp.bfloat16)] * pieces + [TOKEN],
        scratch_shapes=[pltpu.VMEM((count * width, 2 * rows), jnp.bfloat16)],
        compiler_params=params(40, "arbitrary"),
        cost_estimate=LITTLE,
        name="term_x" if by_x else "term_y",
    )(place, mine, theirs, own, sib, *small, after)


def add_x_kernel(*refs):
    parts, (_, keep_ref, send_ref) = refs[:-3], refs[-3:]
    width = keep_ref.shape[0]
    total = parts[0][...].astype(jnp.float32)
    for part in parts[1:]:
        total += part[...].astype(jnp.float32)
    keep_ref[...] = total[:width]
    send_ref[...] = total[width:].astype(jnp.bfloat16)


def add_y_kernel(first_low, first_high, second_low, second_high, after_ref, *outs):
    width = outs[0].shape[0]
    for half, (first, second) in enumerate(((first_low, second_low), (first_high, second_high))):
        total = first[...].astype(jnp.float32) + second[...].astype(jnp.float32)
        for k in range(2):
            out = outs[2 * half + k]
            out[...] = total[k * width : (k + 1) * width].astype(out.dtype)


def add_call(kernel, parts, width, sends, extra=()):
    cols = parts[0].shape[1]
    tile = lambda rows: pl.BlockSpec((rows, cols // 2), lambda n: (0, n))
    return pl.pallas_call(
        kernel,
        grid=(2,),
        in_specs=[tile(a.shape[0]) for a in parts] + [ANY] * len(extra),
        out_specs=[tile(width)] * (sends + 1),
        out_shape=[jax.ShapeDtypeStruct((width, cols), jnp.float32)]
        + [jax.ShapeDtypeStruct((width, cols), jnp.bfloat16)] * sends,
        compiler_params=params(56, "arbitrary"),
        cost_estimate=LITTLE,
        name="add",
    )(*parts, *extra)


def grads_kernel(place_ref, grad_ref, same_ref, other_ref, gate_ref, up_ref, *refs):
    gate_grad_ref, up_grad_ref, token_ref, weight_ref = refs[-4:]
    width = weight_ref.shape[0] // (NX * NY * NC)
    y_index = place_ref[2]
    for k in range(NX * NC):
        x, core = k // NC, k % NC
        for ref, y in ((same_ref, y_index), (other_ref, 1 - y_index)):
            start = pl.multiple_of(((x * NY + y) * NC + core) * width, width)
            weight_ref[pl.ds(start, width), :] = ref[pl.ds(k * width, width), :]
    token_ref[...] = jnp.zeros_like(token_ref)
    hidden_grad = jnp.dot(grad_ref[...], weight_ref[...], preferred_element_type=jnp.float32)
    gelu_value, gelu_slope = gelu_parts(gate_ref[...].astype(jnp.float32))
    gate_grad_ref[...] = (hidden_grad * up_ref[...].astype(jnp.float32) * gelu_slope).astype(
        jnp.bfloat16
    )
    up_grad_ref[...] = (hidden_grad * gelu_value).astype(jnp.bfloat16)


def grads_call(place, grad, weights, gate, up, after, first, steps, held):
    rows, depth = grad.shape
    cols = gate.shape[1]
    weight = pl.BlockSpec((depth // 2, TILE), lambda n: (0, n + first))
    tile = pl.BlockSpec((rows, TILE), lambda n: (0, n + first))
    return pl.pallas_call(
        grads_kernel,
        grid=(steps,),
        in_specs=[
            SMEM,
            pl.BlockSpec((rows, depth), lambda n: (0, 0)),
            weight,
            weight,
            tile,
            tile,
            ANY,
        ]
        + [ANY] * len(held),
        out_specs=[tile, tile, pl.BlockSpec(TOKEN.shape, lambda n: (0, 0))],
        out_shape=[jax.ShapeDtypeStruct((rows, cols), jnp.bfloat16)] * 2 + [TOKEN],
        scratch_shapes=[pltpu.VMEM((depth, TILE), jnp.bfloat16)],
        input_output_aliases={7 + k: k for k in range(len(held))},
        compiler_params=params(56, "arbitrary"),
        cost_estimate=LITTLE,
        name="grads",
    )(place, grad, *weights, gate, up, after, *held)


def update_kernel(scale, own_x, got_x, own_y, *refs):
    got_y, noise_ref, out_ref = refs[:-3], refs[-3], refs[-1]
    split = own_x.shape[1]
    total = own_x[...] + got_x[...].astype(jnp.float32)
    out_ref[:, :split] = scale * total + noise_ref[:, :split]
    total = own_y[...]
    for block in got_y:
        total += block[...].astype(jnp.float32)
    out_ref[:, split:] = scale * total + noise_ref[:, split:]


def update_call(scale, parts, noise, after):
    rows, cols = noise.shape
    spec = lambda a: pl.BlockSpec((rows // 3, a.shape[1]), lambda n: (n, 0))
    return pl.pallas_call(
        functools.partial(update_kernel, scale),
        grid=(3,),
        in_specs=[spec(a) for a in parts] + [spec(noise), ANY],
        out_specs=spec(noise),
        out_shape=jax.ShapeDtypeStruct(noise.shape, jnp.float32),
        compiler_params=params(24, "arbitrary"),
        cost_estimate=LITTLE,
        name="update",
    )(*parts, noise, after)


def local(gate_pre, up_pre, out_grad, down_weight, token_user, noise):
    users_group = USR_DEV * NP * NZ
    groups = NX * NY * NC
    clip_bound = 0.5 * math.sqrt(SLOTS * F * D)
    width = D // groups
    rows = gate_pre.shape[0]
    core = lax.axis_index("c")
    x_index = lax.axis_index("x")
    y_index = lax.axis_index("yh")

    weight = down_weight.T
    weight_other = lax.ppermute(weight, "yh", shift(NY, 1))
    pair = lax.axis_index("yl")
    ring = lax.axis_index("z")
    other = lax.ppermute(out_grad, "yl", shift(NP, 1))
    left = lax.ppermute(out_grad, "z", shift(NZ, 1))
    right = lax.ppermute(out_grad, "z", shift(NZ, -1))
    far = lax.ppermute(out_grad, "z", shift(NZ, 2))

    hidden = hidden_call(gate_pre, up_pre)
    other, left, right, far, hidden, weight_other = lax.optimization_barrier(
        (other, left, right, far, hidden, weight_other)
    )
    weights = [
        lax.all_gather(part, ("x", "c"), axis=0, tiled=True) for part in (weight, weight_other)
    ]
    other_left = lax.ppermute(other, "z", shift(NZ, 1))
    other_right = lax.ppermute(other, "z", shift(NZ, -1))
    other_far = lax.ppermute(far, "yl", shift(NP, 1))

    hidden_sib = lax.ppermute(hidden, "c", shift(NC, 1))
    user_row = token_user.reshape(1, rows)
    user_sib = lax.ppermute(user_row, "c", shift(NC, 1))
    gram = hidden_gram_call(hidden, token_user, user_row)

    other_left, other_right, other_far, user_sib, gram = lax.optimization_barrier(
        (other_left, other_right, other_far, user_sib, gram)
    )
    pieces = [out_grad, left, right, far, other, other_left, other_right, other_far]
    place = [
        (at * NZ + (ring + step) % NZ) * out_grad.shape[0]
        for at in (pair, 1 - pair)
        for step in (0, 3, 1, 2)
    ]
    place = jnp.stack([core, x_index, y_index, *place]).astype(jnp.int32)
    grad_rows, squares = grad_gram_call(place, pieces, gram, user_row, users_group)
    mine, others = transpose_call(place, grad_rows, width)
    squares_sib = lax.ppermute(squares, "c", shift(NC, 1))
    squares_sib, others = lax.optimization_barrier((squares_sib, others))
    theirs = lax.ppermute(others, "c", shift(NC, 1))
    squares = jnp.concatenate([squares, squares_sib], axis=0)
    squares = squares + lax.ppermute(squares, "yl", shift(NP, 1))
    squares = squares + lax.ppermute(squares, "z", [(0, 1), (1, 0), (2, 3), (3, 2)])
    more = lax.ppermute(squares, "z", [(0, 3), (3, 0), (1, 2), (2, 1)])

    cols = hidden.shape[1]
    split = (cols // TILE + 1) // 2 * TILE
    term = lambda by_x, start, count, after: term_call(
        by_x, place, mine, theirs, hidden, hidden_sib, squares, more, user_row, user_sib,
        clip_bound, start, count, after,
    )
    *term_x, done = term(True, 0, split, place)
    got_x = {dx: lax.ppermute(term_x[dx], "x", shift(NX, dx)) for dx in (2, 1, 3)}
    *term_y, done = term(False, split, cols - split, done)
    got_y = [lax.ppermute(part, "yh", shift(NY, 1)) for part in term_y[2:]]

    steps = cols // TILE
    early = (2 * steps) // 3
    *held, done = grads_call(place, grad_rows, weights, gate_pre, up_pre, done, 0, early, ())

    keep_x, send_x = add_call(
        add_x_kernel, [term_x[0], *got_x.values()], width, 1, (done,)
    )
    last_x = lax.ppermute(send_x, "yh", shift(NY, 1))
    keep_y, *send_y = add_call(add_y_kernel, [*term_y[:2], *got_y], width, NX - 1, (done,))
    last_y = [lax.ppermute(send_y[dx - 1], "x", shift(NX, dx)) for dx in (2, 1, 3)]

    gate_grad, up_grad, done = grads_call(
        place, grad_rows, weights, gate_pre, up_pre, send_y[0], early, steps - early, held
    )
    scale = math.sqrt(F * D) / (users_group * groups * clip_bound)
    weight_update = update_call(
        scale, [keep_x, last_x, keep_y, *last_y], noise.T, done
    ).T
    return (gate_grad, up_grad, weight_update)


def solution(mesh):
    fine = Mesh(mesh.devices.reshape(NX, NY, NC, NP, NZ), ("x", "yh", "c", "yl", "z"))
    fsdp = ("x", "yh", "c")
    user = ("yl", "z")
    return jax.shard_map(
        local,
        mesh=fine,
        in_specs=(
            P(fsdp, user),
            P(fsdp, user),
            P(fsdp + user, None),
            P(user, fsdp),
            P(fsdp, None),
            P(user, fsdp),
        ),
        out_specs=(P(fsdp, user), P(fsdp, user), P(user, fsdp)),
        check_vma=False,
    )
```

```python
import functools
import math

import jax
import jax.numpy as jnp
from jax import lax
from jax.experimental import pallas as pl
from jax.experimental.pallas import tpu as pltpu
from jax.sharding import Mesh, PartitionSpec as P

D = 2304
F = 18432
SLOTS = 128
USR_DEV = 2
NX, NY, NC, NP, NZ = 4, 2, 2, 2, 4
TILE = 256
MIB = 2**20

root_two_pi = math.sqrt(2.0 / math.pi)
VMEM = pl.BlockSpec(memory_space=pltpu.VMEM)
SMEM = pl.BlockSpec(memory_space=pltpu.SMEM)
ANY = pl.BlockSpec(memory_space=pl.ANY)


def gelu_parts(gate):
    square = gate * gate
    tanh_value = jnp.tanh(gate * (root_two_pi + (root_two_pi * 0.044715) * square))
    share = 0.5 + 0.5 * tanh_value
    gelu_slope = share + (0.5 * gate) * (1.0 - tanh_value * tanh_value) * (
        root_two_pi + (root_two_pi * 3.0 * 0.044715) * square
    )
    return (gate * share, gelu_slope)


def shift(count, by):
    return [(i, (i + by) % count) for i in range(count)]


LITTLE = pl.CostEstimate(flops=1, bytes_accessed=1, transcendentals=0)
TOKEN = jax.ShapeDtypeStruct((8, 128), jnp.float32)


def params(mib, *semantics):
    return pltpu.CompilerParams(
        vmem_limit_bytes=mib * MIB, dimension_semantics=semantics or None
    )


def hidden_kernel(gate_ref, up_ref, hidden_ref):
    gelu_value, _ = gelu_parts(gate_ref[...].astype(jnp.float32))
    hidden_ref[...] = (gelu_value * up_ref[...].astype(jnp.float32)).astype(jnp.bfloat16)


def hidden_call(gate, up):
    rows, cols = gate.shape
    spec = pl.BlockSpec((TILE // 2, cols), lambda i: (i, 0))
    return pl.pallas_call(
        hidden_kernel,
        grid=(2 * rows // TILE,),
        in_specs=[spec, spec],
        out_specs=spec,
        out_shape=jax.ShapeDtypeStruct(gate.shape, jnp.bfloat16),
        compiler_params=params(40, "arbitrary"),
        cost_estimate=LITTLE,
        name="hidden",
    )(gate, up)


def tiles_of(rows):
    count = rows // TILE
    return [(i, j) for i in range(count) for j in range(i, count)]


def outer(left, right):
    return lax.dot_general(
        left, right, (((1,), (1,)), ((), ())), preferred_element_type=jnp.float32
    )


def hidden_gram_kernel(hidden_ref, user_ref, user_row_ref, gram_ref):
    for k, (i, j) in enumerate(tiles_of(hidden_ref.shape[0])):
        first, second = pl.ds(i * TILE, TILE), pl.ds(j * TILE, TILE)
        tile = outer(hidden_ref[first, :], hidden_ref[second, :])
        same = user_ref[first, :] == user_row_ref[:, second]
        gram_ref[k] = jnp.where(same, tile if i == j else 2.0 * tile, 0.0)


def hidden_gram_call(hidden, user, user_row):
    rows, cols = hidden.shape
    count = len(tiles_of(rows))
    return pl.pallas_call(
        hidden_gram_kernel,
        in_specs=[VMEM, VMEM, VMEM],
        out_specs=VMEM,
        out_shape=jax.ShapeDtypeStruct((count, TILE, TILE), jnp.float32),
        compiler_params=params(24),
        cost_estimate=LITTLE,
        name="hidden_gram",
    )(hidden, user, user_row)


def grad_gram_kernel(place_ref, *refs):
    count = len(refs) - 5
    pieces = refs[:count]
    gram_ref, user_row_ref, grad_ref, squares_ref, sems = refs[count:]
    copies = []
    for k, piece in enumerate(pieces):
        size = piece.shape[0]
        start = pl.multiple_of(place_ref[k + 3], size)
        copies.append(pltpu.make_async_copy(piece, grad_ref.at[pl.ds(start, size)], sems.at[k]))
    for copy in copies:
        copy.start()
    for copy in copies:
        copy.wait()
    rows = grad_ref.shape[0]
    terms = [None] * (rows // TILE)
    for k, (i, j) in enumerate(tiles_of(rows)):
        tile = outer(grad_ref[pl.ds(i * TILE, TILE), :], grad_ref[pl.ds(j * TILE, TILE), :])
        term = jnp.sum(tile * gram_ref[k], axis=0, keepdims=True)
        terms[j] = term if terms[j] is None else terms[j] + term
    terms = jnp.concatenate(terms, axis=1)
    users = lax.broadcasted_iota(jnp.int32, (squares_ref.shape[0], rows), 0)
    chosen = jnp.where(users == user_row_ref[...], terms, 0.0)
    squares_ref[...] = jnp.broadcast_to(
        jnp.sum(chosen, axis=1, keepdims=True), squares_ref.shape
    )


def grad_gram_call(place, pieces, gram, user_row, users_group):
    rows, cols = user_row.shape[1], pieces[0].shape[1]
    return pl.pallas_call(
        grad_gram_kernel,
        in_specs=[SMEM] + [ANY] * len(pieces) + [VMEM] * 2,
        out_specs=[VMEM] * 2,
        out_shape=[
            jax.ShapeDtypeStruct((rows, cols), jnp.bfloat16),
            jax.ShapeDtypeStruct((users_group, 128), jnp.float32),
        ],
        scratch_shapes=[pltpu.SemaphoreType.DMA((len(pieces),))],
        compiler_params=params(40),
        cost_estimate=LITTLE,
        name="grad_gram",
    )(place, *pieces, gram, user_row)


def transpose_kernel(place_ref, grad_ref, mine_ref, other_ref):
    core = place_ref[0]
    count, width, _ = mine_ref.shape
    turned = grad_ref[...].T
    for k in range(count):
        first, second = (turned[(2 * k + i) * width : (2 * k + i + 1) * width] for i in range(2))
        mine_ref[k] = jnp.where(core == 0, first, second)
        other_ref[k] = jnp.where(core == 0, second, first)


def transpose_call(place, grad, width):
    rows, cols = grad.shape
    count = cols // width // NC
    out = pl.BlockSpec((count // 2, width, rows), lambda i: (i, 0, 0))
    return pl.pallas_call(
        transpose_kernel,
        grid=(2,),
        in_specs=[SMEM, pl.BlockSpec((rows, cols // 2), lambda i: (0, i))],
        out_specs=[out, out],
        out_shape=[jax.ShapeDtypeStruct((count, width, rows), grad.dtype)] * 2,
        compiler_params=params(40, "arbitrary"),
        cost_estimate=LITTLE,
        name="transpose",
    )(place, grad)


def scaled_tile(
    clip_bound, place_ref, mine_ref, theirs_ref, squares_ref, more_ref, user_refs, hidden_refs,
    scaled_ref
):
    width, rows = mine_ref.shape[1:]
    count = squares_ref.shape[0] // 2
    ids = lax.broadcasted_iota(jnp.int32, (count, rows), 0)
    x_index, y_index = place_ref[1], place_ref[2]
    total = None
    for group, ref in enumerate((mine_ref, theirs_ref)):
        inside = pl.ds(group * count, count)
        squares = squares_ref[inside, 0:1] + more_ref[inside, 0:1]
        factor = clip_bound / jnp.maximum(jnp.sqrt(squares), clip_bound)
        chosen = jnp.where(ids == user_refs[group][...], factor, 0.0)
        row_factor = jnp.sum(chosen, axis=0, keepdims=True)
        for start in range(0, rows, 2 * TILE):
            parts = []
            for dx in range(NX):
                for dy in range(NY):
                    index = ((x_index + dx) % NX) * NY + (y_index + dy) % NY
                    block = ref[index, :, start : start + 2 * TILE].astype(jnp.float32)
                    parts.append(
                        (block * row_factor[:, start : start + 2 * TILE]).astype(jnp.bfloat16)
                    )
            scaled = jnp.concatenate(parts, axis=0)
            scaled_ref[:, pl.ds(group * rows + start, 2 * TILE)] = scaled
            part = jnp.dot(
                scaled,
                hidden_refs[group][pl.ds(start, 2 * TILE), :],
                preferred_element_type=jnp.float32,
            )
            total = part if total is None else total + part
    return total


def term_kernel(
    clip_bound, by_x, place_ref, mine_ref, theirs_ref, own_ref, sib_ref, squares_ref, more_ref,
    user_ref, user_sib_ref, after_ref, *refs
):
    outs, token_ref, scaled_ref = refs[:-2], refs[-2], refs[-1]
    token_ref[...] = jnp.zeros_like(token_ref)

    rows = own_ref.shape[0]

    def put(total):
        total = total.astype(jnp.bfloat16)
        size = mine_ref.shape[1]
        for dx in range(NX):
            for dy in range(NY):
                out, at = (outs[dx], dy) if by_x else (outs[2 * dy + dx // 2], dx % 2)
                out[pl.ds(at * size, size), :] = total[(dx * NY + dy) * size :][:size]

    @pl.when(pl.program_id(0) == 0)
    def _():
        put(
            scaled_tile(
                clip_bound, place_ref, mine_ref, theirs_ref, squares_ref, more_ref,
                (user_ref, user_sib_ref), (own_ref, sib_ref), scaled_ref,
            )
        )

    @pl.when(pl.program_id(0) > 0)
    def _():
        total = jnp.dot(scaled_ref[:, :rows], own_ref[...], preferred_element_type=jnp.float32)
        total += jnp.dot(scaled_ref[:, rows:], sib_ref[...], preferred_element_type=jnp.float32)
        put(total)


def term_call(
    by_x, place, mine, theirs, own, sib, squares, more, user_row, user_sib, clip_bound, start, cols,
    after
):
    count, width, rows = mine.shape
    whole = lambda a: pl.BlockSpec(a.shape, lambda n: (0,) * a.ndim)
    hidden = pl.BlockSpec((rows, TILE), lambda n: (0, n + start // TILE))
    pieces = NX if by_x else 2 * NY
    size = count * width // pieces
    small = [squares, more, user_row, user_sib]
    return pl.pallas_call(
        functools.partial(term_kernel, clip_bound, by_x),
        grid=(cols // TILE,),
        in_specs=[SMEM, whole(mine), whole(theirs), hidden, hidden] + [whole(a) for a in small] + [ANY],
        out_specs=[pl.BlockSpec((size, TILE), lambda n: (0, n))] * pieces + [whole(TOKEN)],
        out_shape=[jax.ShapeDtypeStruct((size, cols), jnp.bfloat16)] * pieces + [TOKEN],
        scratch_shapes=[pltpu.VMEM((count * width, 2 * rows), jnp.bfloat16)],
        compiler_params=params(40, "arbitrary"),
        cost_estimate=LITTLE,
        name="term_x" if by_x else "term_y",
    )(place, mine, theirs, own, sib, *small, after)


def add_x_kernel(*refs):
    parts, (_, keep_ref, send_ref) = refs[:-3], refs[-3:]
    width = keep_ref.shape[0]
    total = parts[0][...].astype(jnp.float32)
    for part in parts[1:]:
        total += part[...].astype(jnp.float32)
    keep_ref[...] = total[:width]
    send_ref[...] = total[width:].astype(jnp.bfloat16)


def add_y_kernel(first_low, first_high, second_low, second_high, after_ref, *outs):
    width = outs[0].shape[0]
    for half, (first, second) in enumerate(((first_low, second_low), (first_high, second_high))):
        total = first[...].astype(jnp.float32) + second[...].astype(jnp.float32)
        for k in range(2):
            out = outs[2 * half + k]
            out[...] = total[k * width : (k + 1) * width].astype(out.dtype)


def add_call(kernel, parts, width, sends, extra=()):
    cols = parts[0].shape[1]
    tile = lambda rows: pl.BlockSpec((rows, cols // 2), lambda n: (0, n))
    return pl.pallas_call(
        kernel,
        grid=(2,),
        in_specs=[tile(a.shape[0]) for a in parts] + [ANY] * len(extra),
        out_specs=[tile(width)] * (sends + 1),
        out_shape=[jax.ShapeDtypeStruct((width, cols), jnp.float32)]
        + [jax.ShapeDtypeStruct((width, cols), jnp.bfloat16)] * sends,
        compiler_params=params(56, "arbitrary"),
        cost_estimate=LITTLE,
        name="add",
    )(*parts, *extra)


def grads_kernel(place_ref, grad_ref, same_ref, other_ref, gate_ref, up_ref, *refs):
    gate_grad_ref, up_grad_ref, token_ref, weight_ref = refs[-4:]
    width = weight_ref.shape[0] // (NX * NY * NC)
    y_index = place_ref[2]
    for k in range(NX * NC):
        x, core = k // NC, k % NC
        for ref, y in ((same_ref, y_index), (other_ref, 1 - y_index)):
            start = pl.multiple_of(((x * NY + y) * NC + core) * width, width)
            weight_ref[pl.ds(start, width), :] = ref[pl.ds(k * width, width), :]
    token_ref[...] = jnp.zeros_like(token_ref)
    hidden_grad = jnp.dot(grad_ref[...], weight_ref[...], preferred_element_type=jnp.float32)
    gelu_value, gelu_slope = gelu_parts(gate_ref[...].astype(jnp.float32))
    gate_grad_ref[...] = (hidden_grad * up_ref[...].astype(jnp.float32) * gelu_slope).astype(
        jnp.bfloat16
    )
    up_grad_ref[...] = (hidden_grad * gelu_value).astype(jnp.bfloat16)


def grads_call(place, grad, weights, gate, up, after, first, steps, held):
    rows, depth = grad.shape
    cols = gate.shape[1]
    weight = pl.BlockSpec((depth // 2, TILE), lambda n: (0, n + first))
    tile = pl.BlockSpec((rows, TILE), lambda n: (0, n + first))
    return pl.pallas_call(
        grads_kernel,
        grid=(steps,),
        in_specs=[
            SMEM,
            pl.BlockSpec((rows, depth), lambda n: (0, 0)),
            weight,
            weight,
            tile,
            tile,
            ANY,
        ]
        + [ANY] * len(held),
        out_specs=[tile, tile, pl.BlockSpec(TOKEN.shape, lambda n: (0, 0))],
        out_shape=[jax.ShapeDtypeStruct((rows, cols), jnp.bfloat16)] * 2 + [TOKEN],
        scratch_shapes=[pltpu.VMEM((depth, TILE), jnp.bfloat16)],
        input_output_aliases={7 + k: k for k in range(len(held))},
        compiler_params=params(52, "arbitrary"),
        cost_estimate=LITTLE,
        name="grads",
    )(place, grad, *weights, gate, up, after, *held)


def update_kernel(scale, own_x, got_x, own_y, *refs):
    got_y, noise_ref, out_ref = refs[:-3], refs[-3], refs[-1]
    split = own_x.shape[1]
    total = own_x[...] + got_x[...].astype(jnp.float32)
    out_ref[:, :split] = scale * total + noise_ref[:, :split]
    total = own_y[...]
    for block in got_y:
        total += block[...].astype(jnp.float32)
    out_ref[:, split:] = scale * total + noise_ref[:, split:]


def update_call(scale, parts, noise, after):
    rows, cols = noise.shape
    spec = lambda a: pl.BlockSpec((rows // 3, a.shape[1]), lambda n: (n, 0))
    return pl.pallas_call(
        functools.partial(update_kernel, scale),
        grid=(3,),
        in_specs=[spec(a) for a in parts] + [spec(noise), ANY],
        out_specs=spec(noise),
        out_shape=jax.ShapeDtypeStruct(noise.shape, jnp.float32),
        compiler_params=params(24, "arbitrary"),
        cost_estimate=LITTLE,
        name="update",
    )(*parts, noise, after)


def local(gate_pre, up_pre, out_grad, down_weight, token_user, noise):
    users_group = USR_DEV * NP * NZ
    groups = NX * NY * NC
    clip_bound = 0.5 * math.sqrt(SLOTS * F * D)
    width = D // groups
    rows = gate_pre.shape[0]
    core = lax.axis_index("c")
    x_index = lax.axis_index("x")
    y_index = lax.axis_index("yh")

    weight = down_weight.T
    weight_other = lax.ppermute(weight, "yh", shift(NY, 1))
    pair = lax.axis_index("yl")
    ring = lax.axis_index("z")
    other = lax.ppermute(out_grad, "yl", shift(NP, 1))
    left = lax.ppermute(out_grad, "z", shift(NZ, 1))
    right = lax.ppermute(out_grad, "z", shift(NZ, -1))
    far = lax.ppermute(out_grad, "z", shift(NZ, 2))

    hidden = hidden_call(gate_pre, up_pre)
    other, left, right, far, hidden, weight_other = lax.optimization_barrier(
        (other, left, right, far, hidden, weight_other)
    )
    weights = [
        lax.all_gather(part, ("x", "c"), axis=0, tiled=True) for part in (weight, weight_other)
    ]
    other_left = lax.ppermute(other, "z", shift(NZ, 1))
    other_right = lax.ppermute(other, "z", shift(NZ, -1))
    other_far = lax.ppermute(far, "yl", shift(NP, 1))

    hidden_sib = lax.ppermute(hidden, "c", shift(NC, 1))
    user_row = token_user.reshape(1, rows)
    user_sib = lax.ppermute(user_row, "c", shift(NC, 1))
    gram = hidden_gram_call(hidden, token_user, user_row)

    other_left, other_right, other_far, user_sib, gram = lax.optimization_barrier(
        (other_left, other_right, other_far, user_sib, gram)
    )
    pieces = [out_grad, left, right, far, other, other_left, other_right, other_far]
    place = [
        (at * NZ + (ring + step) % NZ) * out_grad.shape[0]
        for at in (pair, 1 - pair)
        for step in (0, 3, 1, 2)
    ]
    place = jnp.stack([core, x_index, y_index, *place]).astype(jnp.int32)
    grad_rows, squares = grad_gram_call(place, pieces, gram, user_row, users_group)
    mine, others = transpose_call(place, grad_rows, width)
    squares_sib = lax.ppermute(squares, "c", shift(NC, 1))
    squares_sib, others = lax.optimization_barrier((squares_sib, others))
    theirs = lax.ppermute(others, "c", shift(NC, 1))
    squares = jnp.concatenate([squares, squares_sib], axis=0)
    squares = squares + lax.ppermute(squares, "yl", shift(NP, 1))
    squares = squares + lax.ppermute(squares, "z", [(0, 1), (1, 0), (2, 3), (3, 2)])
    more = lax.ppermute(squares, "z", [(0, 3), (3, 0), (1, 2), (2, 1)])

    cols = hidden.shape[1]
    split = (cols // TILE + 1) // 2 * TILE
    term = lambda by_x, start, count, after: term_call(
        by_x, place, mine, theirs, hidden, hidden_sib, squares, more, user_row, user_sib,
        clip_bound, start, count, after,
    )
    *term_x, done = term(True, 0, split, place)
    got_x = {dx: lax.ppermute(term_x[dx], "x", shift(NX, dx)) for dx in (2, 1, 3)}
    *term_y, done = term(False, split, cols - split, done)
    got_y = [lax.ppermute(part, "yh", shift(NY, 1)) for part in term_y[2:]]

    steps = cols // TILE
    early = (2 * steps) // 3 + 1
    *held, done = grads_call(place, grad_rows, weights, gate_pre, up_pre, done, 0, early, ())

    keep_x, send_x = add_call(
        add_x_kernel, [term_x[0], *got_x.values()], width, 1, (done,)
    )
    last_x = lax.ppermute(send_x, "yh", shift(NY, 1))
    keep_y, *send_y = add_call(add_y_kernel, [*term_y[:2], *got_y], width, NX - 1, (done,))
    last_y = [lax.ppermute(send_y[dx - 1], "x", shift(NX, dx)) for dx in (2, 1, 3)]

    gate_grad, up_grad, done = grads_call(
        place, grad_rows, weights, gate_pre, up_pre, send_y[0], early, steps - early, held
    )
    scale = math.sqrt(F * D) / (users_group * groups * clip_bound)
    weight_update = update_call(
        scale, [keep_x, last_x, keep_y, *last_y], noise.T, done
    ).T
    return (gate_grad, up_grad, weight_update)


def solution(mesh):
    fine = Mesh(mesh.devices.reshape(NX, NY, NC, NP, NZ), ("x", "yh", "c", "yl", "z"))
    fsdp = ("x", "yh", "c")
    user = ("yl", "z")
    return jax.shard_map(
        local,
        mesh=fine,
        in_specs=(
            P(fsdp, user),
            P(fsdp, user),
            P(fsdp + user, None),
            P(user, fsdp),
            P(fsdp, None),
            P(user, fsdp),
        ),
        out_specs=(P(fsdp, user), P(fsdp, user), P(user, fsdp)),
        check_vma=False,
    )
```

```python
import functools
import math

import jax
import jax.numpy as jnp
from jax import lax
from jax.experimental import pallas as pl
from jax.experimental.pallas import tpu as pltpu
from jax.sharding import Mesh, PartitionSpec as P

D = 2304
F = 18432
SLOTS = 128
USR_DEV = 2
NX, NY, NC, NP, NZ = 4, 2, 2, 2, 4
TILE = 256
MIB = 2**20

root_two_pi = math.sqrt(2.0 / math.pi)
VMEM = pl.BlockSpec(memory_space=pltpu.VMEM)
SMEM = pl.BlockSpec(memory_space=pltpu.SMEM)
ANY = pl.BlockSpec(memory_space=pl.ANY)


def gelu_parts(gate):
    square = gate * gate
    tanh_value = jnp.tanh(gate * (root_two_pi + (root_two_pi * 0.044715) * square))
    share = 0.5 + 0.5 * tanh_value
    gelu_slope = share + (0.5 * gate) * (1.0 - tanh_value * tanh_value) * (
        root_two_pi + (root_two_pi * 3.0 * 0.044715) * square
    )
    return (gate * share, gelu_slope)


def shift(count, by):
    return [(i, (i + by) % count) for i in range(count)]


LITTLE = pl.CostEstimate(flops=1, bytes_accessed=1, transcendentals=0)
TOKEN = jax.ShapeDtypeStruct((8, 128), jnp.float32)


def params(mib, *semantics):
    return pltpu.CompilerParams(
        vmem_limit_bytes=mib * MIB, dimension_semantics=semantics or None
    )


def hidden_kernel(gate_ref, up_ref, hidden_ref):
    gelu_value, _ = gelu_parts(gate_ref[...].astype(jnp.float32))
    hidden_ref[...] = (gelu_value * up_ref[...].astype(jnp.float32)).astype(jnp.bfloat16)


def hidden_call(gate, up):
    rows, cols = gate.shape
    spec = pl.BlockSpec((TILE // 2, cols), lambda i: (i, 0))
    return pl.pallas_call(
        hidden_kernel,
        grid=(2 * rows // TILE,),
        in_specs=[spec, spec],
        out_specs=spec,
        out_shape=jax.ShapeDtypeStruct(gate.shape, jnp.bfloat16),
        compiler_params=params(16, "arbitrary"),
        cost_estimate=LITTLE,
        name="hidden",
    )(gate, up)


def outer(left, right):
    return lax.dot_general(
        left, right, (((1,), (1,)), ((), ())), preferred_element_type=jnp.float32
    )


def starts_of(place_ref, size):
    return [pl.multiple_of(place_ref[3 + k], size) for k in range(NP * NZ)]


def hidden_gram_kernel(
    place_ref, hidden_ref, user_ref, user_row_ref, ee_ref, la_ref, row_ref, rows, users
):
    size = rows.shape[0] // (NP * NZ)
    early = ee_ref.shape[0]
    for k, start in enumerate(starts_of(place_ref, size)):
        inside = pl.ds(k * size, size)
        rows[inside, :] = hidden_ref[pl.ds(start, size), :]
        users[inside, :] = user_ref[pl.ds(start, size), :]
        row_ref[:, inside] = user_row_ref[:, pl.ds(start, size)]
    gram = outer(rows[:early, :], rows[:early, :])
    ee_ref[...] = jnp.where(users[:early, :] == row_ref[:, :early], gram, 0.0)
    for columns, weight in ((slice(0, early), 2.0), (slice(early, rows.shape[0]), 1.0)):
        gram = weight * outer(rows[early:, :], rows[columns, :])
        la_ref[:, columns] = jnp.where(users[early:, :] == row_ref[:, columns], gram, 0.0)


def hidden_gram_call(place, hidden, user, user_row, early):
    rows, cols = hidden.shape
    late = rows - early
    gram = lambda a, b: jax.ShapeDtypeStruct((a, b), jnp.float32)
    return pl.pallas_call(
        hidden_gram_kernel,
        in_specs=[SMEM, VMEM, VMEM, VMEM],
        out_specs=[VMEM] * 3,
        out_shape=[
            gram(early, early),
            gram(late, rows),
            jax.ShapeDtypeStruct((1, rows), jnp.int32),
        ],
        scratch_shapes=[pltpu.VMEM((rows, cols), jnp.bfloat16), pltpu.VMEM((rows, 1), jnp.int32)],
        compiler_params=params(20),
        cost_estimate=LITTLE,
        name="hidden_gram",
    )(place, hidden, user, user_row)


def gather_blocks(pieces, out_ref, first, sems):
    size = pieces[0].shape[0]
    copies = [
        pltpu.make_async_copy(piece, out_ref.at[pl.ds((first + k) * size, size)], sems.at[k])
        for k, piece in enumerate(pieces)
    ]
    for copy in copies:
        copy.start()
    for copy in copies:
        copy.wait()


def by_user(terms, row, count):
    users = lax.broadcasted_iota(jnp.int32, (count, terms.shape[1]), 0)
    return jnp.sum(jnp.where(users == row, terms, 0.0), axis=1, keepdims=True)


def early_gram_kernel(*refs):
    pieces, (gram_ref, row_ref, out_ref, squares_ref, sems) = refs[:-5], refs[-5:]
    gather_blocks(pieces, out_ref, 0, sems)
    early = gram_ref.shape[0]
    gram = outer(out_ref[:early, :], out_ref[:early, :]) * gram_ref[...]
    terms = jnp.sum(gram, axis=0, keepdims=True)
    squares = by_user(terms, row_ref[:, :early], squares_ref.shape[0])
    squares_ref[...] = jnp.broadcast_to(squares, squares_ref.shape)


def late_gram_kernel(*refs):
    pieces, (gram_ref, row_ref, first_ref, _, out_ref, squares_ref, sems) = refs[:-7], refs[-7:]
    late, rows = gram_ref.shape
    gather_blocks(pieces, out_ref, NP * NZ - len(pieces), sems)
    gram = outer(out_ref[rows - late :, :], out_ref[...]) * gram_ref[...]
    terms = jnp.sum(gram, axis=0, keepdims=True)
    squares_ref[...] = first_ref[...] + by_user(terms, row_ref[...], squares_ref.shape[0])


def gram_call(kernel, pieces, others, users_group, name, held=()):
    size, cols = pieces[0].shape
    inputs = [*pieces, *others, *held]
    return pl.pallas_call(
        kernel,
        in_specs=[ANY] * len(pieces) + [VMEM] * (len(inputs) - len(pieces)),
        out_specs=[VMEM] * 2,
        out_shape=[
            jax.ShapeDtypeStruct((NP * NZ * size, cols), jnp.bfloat16),
            jax.ShapeDtypeStruct((users_group, 128), jnp.float32),
        ],
        scratch_shapes=[pltpu.SemaphoreType.DMA((len(pieces),))],
        input_output_aliases={len(inputs) - 1: 0} if held else {},
        compiler_params=params(20),
        cost_estimate=LITTLE,
        name=name,
    )(*inputs)


def transpose_kernel(place_ref, grad_ref, mine_ref, other_ref):
    core = place_ref[0]
    count, width, rows = mine_ref.shape
    size = rows // (NP * NZ)
    for n, start in enumerate(starts_of(place_ref, size)):
        turned = grad_ref[pl.ds(n * size, size), :].T
        inside = pl.ds(start, size)
        for k in range(count):
            first, second = (
                turned[(2 * k + i) * width : (2 * k + i + 1) * width] for i in range(2)
            )
            mine_ref[k, :, inside] = jnp.where(core == 0, first, second)
            other_ref[k, :, inside] = jnp.where(core == 0, second, first)


def transpose_call(place, grad, width):
    rows, cols = grad.shape
    count = cols // width // NC
    out = pl.BlockSpec((count // 2, width, rows), lambda i: (i, 0, 0))
    return pl.pallas_call(
        transpose_kernel,
        grid=(2,),
        in_specs=[SMEM, pl.BlockSpec((rows, cols // 2), lambda i: (0, i))],
        out_specs=[out, out],
        out_shape=[jax.ShapeDtypeStruct((count, width, rows), grad.dtype)] * 2,
        compiler_params=params(40, "arbitrary"),
        cost_estimate=LITTLE,
        name="transpose",
    )(place, grad)


def scaled_tile(
    clip_bound, place_ref, mine_ref, theirs_ref, squares_ref, more_ref, user_refs, hidden_refs,
    scaled_ref
):
    width, rows = mine_ref.shape[1:]
    count = squares_ref.shape[0] // 2
    ids = lax.broadcasted_iota(jnp.int32, (count, rows), 0)
    x_index, y_index = place_ref[1], place_ref[2]
    total = None
    for group, ref in enumerate((mine_ref, theirs_ref)):
        inside = pl.ds(group * count, count)
        squares = squares_ref[inside, 0:1] + more_ref[inside, 0:1]
        factor = clip_bound / jnp.maximum(jnp.sqrt(squares), clip_bound)
        chosen = jnp.where(ids == user_refs[group][...], factor, 0.0)
        row_factor = jnp.sum(chosen, axis=0, keepdims=True)
        for start in range(0, rows, 2 * TILE):
            parts = []
            for dx in range(NX):
                for dy in range(NY):
                    index = ((x_index + dx) % NX) * NY + (y_index + dy) % NY
                    block = ref[index, :, start : start + 2 * TILE].astype(jnp.float32)
                    parts.append(
                        (block * row_factor[:, start : start + 2 * TILE]).astype(jnp.bfloat16)
                    )
            scaled = jnp.concatenate(parts, axis=0)
            scaled_ref[:, pl.ds(group * rows + start, 2 * TILE)] = scaled
            part = jnp.dot(
                scaled,
                hidden_refs[group][pl.ds(start, 2 * TILE), :],
                preferred_element_type=jnp.float32,
            )
            total = part if total is None else total + part
    return total


def term_kernel(
    clip_bound, by_x, place_ref, mine_ref, theirs_ref, own_ref, sib_ref, squares_ref, more_ref,
    user_ref, user_sib_ref, after_ref, *refs
):
    outs, token_ref, scaled_ref = refs[:-2], refs[-2], refs[-1]
    token_ref[...] = jnp.zeros_like(token_ref)

    rows = own_ref.shape[0]

    def put(total):
        total = total.astype(jnp.bfloat16)
        size = mine_ref.shape[1]
        for dx in range(NX):
            for dy in range(NY):
                out, at = (outs[dx], dy) if by_x else (outs[2 * dy + dx // 2], dx % 2)
                out[pl.ds(at * size, size), :] = total[(dx * NY + dy) * size :][:size]

    @pl.when(pl.program_id(0) == 0)
    def _():
        put(
            scaled_tile(
                clip_bound, place_ref, mine_ref, theirs_ref, squares_ref, more_ref,
                (user_ref, user_sib_ref), (own_ref, sib_ref), scaled_ref,
            )
        )

    @pl.when(pl.program_id(0) > 0)
    def _():
        total = jnp.dot(scaled_ref[:, :rows], own_ref[...], preferred_element_type=jnp.float32)
        total += jnp.dot(scaled_ref[:, rows:], sib_ref[...], preferred_element_type=jnp.float32)
        put(total)


def term_call(
    by_x, place, mine, theirs, own, sib, squares, more, user_row, user_sib, clip_bound, start, cols,
    after
):
    count, width, rows = mine.shape
    whole = lambda a: pl.BlockSpec(a.shape, lambda n: (0,) * a.ndim)
    hidden = pl.BlockSpec((rows, TILE), lambda n: (0, n + start // TILE))
    pieces = NX if by_x else 2 * NY
    size = count * width // pieces
    small = [squares, more, user_row, user_sib]
    return pl.pallas_call(
        functools.partial(term_kernel, clip_bound, by_x),
        grid=(cols // TILE,),
        in_specs=[SMEM, whole(mine), whole(theirs), hidden, hidden] + [whole(a) for a in small] + [ANY],
        out_specs=[pl.BlockSpec((size, TILE), lambda n: (0, n))] * pieces + [whole(TOKEN)],
        out_shape=[jax.ShapeDtypeStruct((size, cols), jnp.bfloat16)] * pieces + [TOKEN],
        scratch_shapes=[pltpu.VMEM((count * width, 2 * rows), jnp.bfloat16)],
        compiler_params=params(40, "arbitrary"),
        cost_estimate=LITTLE,
        name="term_x" if by_x else "term_y",
    )(place, mine, theirs, own, sib, *small, after)


def add_x_kernel(*refs):
    parts, (_, keep_ref, send_ref) = refs[:-3], refs[-3:]
    width = keep_ref.shape[0]
    total = parts[0][...].astype(jnp.float32)
    for part in parts[1:]:
        total += part[...].astype(jnp.float32)
    keep_ref[...] = total[:width]
    send_ref[...] = total[width:].astype(jnp.bfloat16)


def add_y_kernel(first_low, first_high, second_low, second_high, after_ref, *outs):
    width = outs[0].shape[0]
    for half, (first, second) in enumerate(((first_low, second_low), (first_high, second_high))):
        total = first[...].astype(jnp.float32) + second[...].astype(jnp.float32)
        for k in range(2):
            out = outs[2 * half + k]
            out[...] = total[k * width : (k + 1) * width].astype(out.dtype)


def add_call(kernel, parts, width, sends, extra=()):
    cols = parts[0].shape[1]
    tile = lambda rows: pl.BlockSpec((rows, cols // 2), lambda n: (0, n))
    return pl.pallas_call(
        kernel,
        grid=(2,),
        in_specs=[tile(a.shape[0]) for a in parts] + [ANY] * len(extra),
        out_specs=[tile(width)] * (sends + 1),
        out_shape=[jax.ShapeDtypeStruct((width, cols), jnp.float32)]
        + [jax.ShapeDtypeStruct((width, cols), jnp.bfloat16)] * sends,
        compiler_params=params(56, "arbitrary"),
        cost_estimate=LITTLE,
        name="add",
    )(*parts, *extra)


def grads_kernel(place_ref, blocks_ref, same_ref, other_ref, gate_ref, up_ref, *refs):
    gate_grad_ref, up_grad_ref, token_ref, grad_ref, weight_ref = refs[-5:]

    @pl.when(pl.program_id(0) == 0)
    def _():
        size = grad_ref.shape[0] // (NP * NZ)
        for k, start in enumerate(starts_of(place_ref, size)):
            grad_ref[pl.ds(start, size), :] = blocks_ref[pl.ds(k * size, size), :]

    width = weight_ref.shape[0] // (NX * NY * NC)
    y_index = place_ref[2]
    for k in range(NX * NC):
        x, core = k // NC, k % NC
        for ref, y in ((same_ref, y_index), (other_ref, 1 - y_index)):
            start = pl.multiple_of(((x * NY + y) * NC + core) * width, width)
            weight_ref[pl.ds(start, width), :] = ref[pl.ds(k * width, width), :]
    token_ref[...] = jnp.zeros_like(token_ref)
    hidden_grad = jnp.dot(grad_ref[...], weight_ref[...], preferred_element_type=jnp.float32)
    gelu_value, gelu_slope = gelu_parts(gate_ref[...].astype(jnp.float32))
    gate_grad_ref[...] = (hidden_grad * up_ref[...].astype(jnp.float32) * gelu_slope).astype(
        jnp.bfloat16
    )
    up_grad_ref[...] = (hidden_grad * gelu_value).astype(jnp.bfloat16)


def grads_call(place, blocks, weights, gate, up, after, first, steps, held):
    rows, cols = gate.shape
    depth = blocks.shape[1]
    weight = pl.BlockSpec((depth // 2, TILE), lambda n: (0, n + first))
    tile = pl.BlockSpec((rows, TILE), lambda n: (0, n + first))
    return pl.pallas_call(
        grads_kernel,
        grid=(steps,),
        in_specs=[
            SMEM,
            pl.BlockSpec((rows, depth), lambda n: (0, 0)),
            weight,
            weight,
            tile,
            tile,
            ANY,
        ]
        + [ANY] * len(held),
        out_specs=[tile, tile, pl.BlockSpec(TOKEN.shape, lambda n: (0, 0))],
        out_shape=[jax.ShapeDtypeStruct((rows, cols), jnp.bfloat16)] * 2 + [TOKEN],
        scratch_shapes=[
            pltpu.VMEM((rows, depth), jnp.bfloat16), pltpu.VMEM((depth, TILE), jnp.bfloat16)
        ],
        input_output_aliases={7 + k: k for k in range(len(held))},
        compiler_params=params(52, "arbitrary"),
        cost_estimate=LITTLE,
        name="grads",
    )(place, blocks, *weights, gate, up, after, *held)


def update_kernel(scale, own_x, got_x, own_y, *refs):
    got_y, noise_ref, out_ref = refs[:-3], refs[-3], refs[-1]
    split = own_x.shape[1]
    total = own_x[...] + got_x[...].astype(jnp.float32)
    out_ref[:, :split] = scale * total + noise_ref[:, :split]
    total = own_y[...]
    for block in got_y:
        total += block[...].astype(jnp.float32)
    out_ref[:, split:] = scale * total + noise_ref[:, split:]


def update_call(scale, parts, noise, after):
    rows, cols = noise.shape
    spec = lambda a: pl.BlockSpec((rows // 3, a.shape[1]), lambda n: (n, 0))
    return pl.pallas_call(
        functools.partial(update_kernel, scale),
        grid=(3,),
        in_specs=[spec(a) for a in parts] + [spec(noise), ANY],
        out_specs=spec(noise),
        out_shape=jax.ShapeDtypeStruct(noise.shape, jnp.float32),
        compiler_params=params(24, "arbitrary"),
        cost_estimate=LITTLE,
        name="update",
    )(*parts, noise, after)


def local(gate_pre, up_pre, out_grad, down_weight, token_user, noise):
    users_group = USR_DEV * NP * NZ
    groups = NX * NY * NC
    clip_bound = 0.5 * math.sqrt(SLOTS * F * D)
    width = D // groups
    rows = gate_pre.shape[0]
    core = lax.axis_index("c")
    x_index = lax.axis_index("x")
    y_index = lax.axis_index("yh")

    weight = down_weight.T
    weight_other = lax.ppermute(weight, "yh", shift(NY, 1))
    pair = lax.axis_index("yl")
    ring = lax.axis_index("z")
    other = lax.ppermute(out_grad, "yl", shift(NP, 1))
    left = lax.ppermute(out_grad, "z", shift(NZ, 1))
    right = lax.ppermute(out_grad, "z", shift(NZ, -1))
    far = lax.ppermute(out_grad, "z", shift(NZ, 2))

    hidden = hidden_call(gate_pre, up_pre)
    other, left, right, far, hidden, weight_other = lax.optimization_barrier(
        (other, left, right, far, hidden, weight_other)
    )
    weights = [
        lax.all_gather(part, ("x", "c"), axis=0, tiled=True) for part in (weight, weight_other)
    ]
    other_left = lax.ppermute(other, "z", shift(NZ, 1))
    other_right = lax.ppermute(other, "z", shift(NZ, -1))
    other_far = lax.ppermute(far, "yl", shift(NP, 1))

    hidden_sib = lax.ppermute(hidden, "c", shift(NC, 1))
    user_row = token_user.reshape(1, rows)
    user_sib = lax.ppermute(user_row, "c", shift(NC, 1))
    place = [
        (at * NZ + (ring + step) % NZ) * out_grad.shape[0]
        for at in (pair, 1 - pair)
        for step in (0, 3, 1, 2)
    ]
    place = jnp.stack([core, x_index, y_index, *place]).astype(jnp.int32)
    pieces = [out_grad, left, right, far, other]
    gram_early, gram_late, user_order = hidden_gram_call(
        place, hidden, token_user, user_row, len(pieces) * out_grad.shape[0]
    )
    blocks, squares = gram_call(
        early_gram_kernel, pieces, [gram_early, user_order], users_group, "early_gram"
    )
    other_left, other_right, other_far, user_sib, squares = lax.optimization_barrier(
        (other_left, other_right, other_far, user_sib, squares)
    )
    blocks, squares = gram_call(
        late_gram_kernel,
        [other_left, other_right, other_far],
        [gram_late, user_order, squares],
        users_group,
        "late_gram",
        (blocks,),
    )
    mine, others = transpose_call(place, blocks, width)
    squares_sib = lax.ppermute(squares, "c", shift(NC, 1))
    squares_sib, others = lax.optimization_barrier((squares_sib, others))
    theirs = lax.ppermute(others, "c", shift(NC, 1))
    squares = jnp.concatenate([squares, squares_sib], axis=0)
    squares = squares + lax.ppermute(squares, "yl", shift(NP, 1))
    squares = squares + lax.ppermute(squares, "z", [(0, 1), (1, 0), (2, 3), (3, 2)])
    more = lax.ppermute(squares, "z", [(0, 3), (3, 0), (1, 2), (2, 1)])

    cols = hidden.shape[1]
    split = (cols // TILE + 1) // 2 * TILE
    term = lambda by_x, start, count, after: term_call(
        by_x, place, mine, theirs, hidden, hidden_sib, squares, more, user_row, user_sib,
        clip_bound, start, count, after,
    )
    *term_x, done = term(True, 0, split, place)
    got_x = {dx: lax.ppermute(term_x[dx], "x", shift(NX, dx)) for dx in (2, 1, 3)}
    *term_y, done = term(False, split, cols - split, done)
    got_y = [lax.ppermute(part, "yh", shift(NY, 1)) for part in term_y[2:]]

    steps = cols // TILE
    split_steps = (2 * steps) // 3 + 1
    *held, done = grads_call(place, blocks, weights, gate_pre, up_pre, done, 0, split_steps, ())

    keep_x, send_x = add_call(
        add_x_kernel, [term_x[0], *got_x.values()], width, 1, (done,)
    )
    last_x = lax.ppermute(send_x, "yh", shift(NY, 1))
    keep_y, *send_y = add_call(add_y_kernel, [*term_y[:2], *got_y], width, NX - 1, (done,))
    last_y = [lax.ppermute(send_y[dx - 1], "x", shift(NX, dx)) for dx in (2, 1, 3)]

    gate_grad, up_grad, done = grads_call(
        place, blocks, weights, gate_pre, up_pre, send_y[0], split_steps, steps - split_steps, held
    )
    scale = math.sqrt(F * D) / (users_group * groups * clip_bound)
    weight_update = update_call(
        scale, [keep_x, last_x, keep_y, *last_y], noise.T, done
    ).T
    return (gate_grad, up_grad, weight_update)


def solution(mesh):
    fine = Mesh(mesh.devices.reshape(NX, NY, NC, NP, NZ), ("x", "yh", "c", "yl", "z"))
    fsdp = ("x", "yh", "c")
    user = ("yl", "z")
    return jax.shard_map(
        local,
        mesh=fine,
        in_specs=(
            P(fsdp, user),
            P(fsdp, user),
            P(fsdp + user, None),
            P(user, fsdp),
            P(fsdp, None),
            P(user, fsdp),
        ),
        out_specs=(P(fsdp, user), P(fsdp, user), P(user, fsdp)),
        check_vma=False,
    )
```

```python
import functools
import math

import jax
import jax.numpy as jnp
from jax import lax
from jax.experimental import pallas as pl
from jax.experimental.pallas import tpu as pltpu
from jax.sharding import Mesh, PartitionSpec as P

D = 2304
F = 18432
SLOTS = 128
USR_DEV = 2
NX, NY, NC, NP, NZ = 4, 2, 2, 2, 4
TILE = 256
MIB = 2**20

root_two_pi = math.sqrt(2.0 / math.pi)
VMEM = pl.BlockSpec(memory_space=pltpu.VMEM)
SMEM = pl.BlockSpec(memory_space=pltpu.SMEM)
ANY = pl.BlockSpec(memory_space=pl.ANY)


def gelu_parts(gate):
    square = gate * gate
    tanh_value = jnp.tanh(gate * (root_two_pi + (root_two_pi * 0.044715) * square))
    share = 0.5 + 0.5 * tanh_value
    gelu_slope = share + (0.5 * gate) * (1.0 - tanh_value * tanh_value) * (
        root_two_pi + (root_two_pi * 3.0 * 0.044715) * square
    )
    return (gate * share, gelu_slope)


def shift(count, by):
    return [(i, (i + by) % count) for i in range(count)]


LITTLE = pl.CostEstimate(flops=1, bytes_accessed=1, transcendentals=0)
TOKEN = jax.ShapeDtypeStruct((8, 128), jnp.float32)


def params(mib, *semantics):
    return pltpu.CompilerParams(
        vmem_limit_bytes=mib * MIB, dimension_semantics=semantics or None
    )


def hidden_kernel(gate_ref, up_ref, hidden_ref):
    gelu_value, _ = gelu_parts(gate_ref[...].astype(jnp.float32))
    hidden_ref[...] = (gelu_value * up_ref[...].astype(jnp.float32)).astype(jnp.bfloat16)


def hidden_call(gate, up):
    rows, cols = gate.shape
    spec = pl.BlockSpec((TILE // 2, cols), lambda i: (i, 0))
    return pl.pallas_call(
        hidden_kernel,
        grid=(2 * rows // TILE,),
        in_specs=[spec, spec],
        out_specs=spec,
        out_shape=jax.ShapeDtypeStruct(gate.shape, jnp.bfloat16),
        compiler_params=params(16, "arbitrary"),
        cost_estimate=LITTLE,
        name="hidden",
    )(gate, up)


def outer(left, right):
    return lax.dot_general(
        left, right, (((1,), (1,)), ((), ())), preferred_element_type=jnp.float32
    )


def starts_of(place_ref, size):
    return [pl.multiple_of(place_ref[3 + k], size) for k in range(NP * NZ)]


def hidden_gram_kernel(
    place_ref, hidden_ref, user_ref, user_row_ref, ee_ref, la_ref, row_ref, rows, users
):
    size = rows.shape[0] // (NP * NZ)
    early = ee_ref.shape[0]
    for k, start in enumerate(starts_of(place_ref, size)):
        inside = pl.ds(k * size, size)
        rows[inside, :] = hidden_ref[pl.ds(start, size), :]
        users[inside, :] = user_ref[pl.ds(start, size), :]
        row_ref[:, inside] = user_row_ref[:, pl.ds(start, size)]
    gram = outer(rows[:early, :], rows[:early, :])
    ee_ref[...] = jnp.where(users[:early, :] == row_ref[:, :early], gram, 0.0)
    for columns, weight in ((slice(0, early), 2.0), (slice(early, rows.shape[0]), 1.0)):
        gram = weight * outer(rows[early:, :], rows[columns, :])
        la_ref[:, columns] = jnp.where(users[early:, :] == row_ref[:, columns], gram, 0.0)


def hidden_gram_call(place, hidden, user, user_row, early):
    rows, cols = hidden.shape
    late = rows - early
    gram = lambda a, b: jax.ShapeDtypeStruct((a, b), jnp.float32)
    return pl.pallas_call(
        hidden_gram_kernel,
        in_specs=[SMEM, VMEM, VMEM, VMEM],
        out_specs=[VMEM] * 3,
        out_shape=[
            gram(early, early),
            gram(late, rows),
            jax.ShapeDtypeStruct((1, rows), jnp.int32),
        ],
        scratch_shapes=[pltpu.VMEM((rows, cols), jnp.bfloat16), pltpu.VMEM((rows, 1), jnp.int32)],
        compiler_params=params(20),
        cost_estimate=LITTLE,
        name="hidden_gram",
    )(place, hidden, user, user_row)


def gather_blocks(pieces, out_ref, first, sems):
    size = pieces[0].shape[0]
    copies = [
        pltpu.make_async_copy(piece, out_ref.at[pl.ds((first + k) * size, size)], sems.at[k])
        for k, piece in enumerate(pieces)
    ]
    for copy in copies:
        copy.start()
    for copy in copies:
        copy.wait()


def by_user(terms, row, count):
    users = lax.broadcasted_iota(jnp.int32, (count, terms.shape[1]), 0)
    return jnp.sum(jnp.where(users == row, terms, 0.0), axis=1, keepdims=True)


def early_gram_kernel(*refs):
    pieces, (gram_ref, row_ref, out_ref, squares_ref, sems) = refs[:-5], refs[-5:]
    gather_blocks(pieces, out_ref, 0, sems)
    early = gram_ref.shape[0]
    gram = outer(out_ref[:early, :], out_ref[:early, :]) * gram_ref[...]
    terms = jnp.sum(gram, axis=0, keepdims=True)
    squares = by_user(terms, row_ref[:, :early], squares_ref.shape[0])
    squares_ref[...] = jnp.broadcast_to(squares, squares_ref.shape)


def late_gram_kernel(*refs):
    pieces, (gram_ref, row_ref, first_ref, _, out_ref, squares_ref, sems) = refs[:-7], refs[-7:]
    late, rows = gram_ref.shape
    gather_blocks(pieces, out_ref, NP * NZ - len(pieces), sems)
    gram = outer(out_ref[rows - late :, :], out_ref[...]) * gram_ref[...]
    terms = jnp.sum(gram, axis=0, keepdims=True)
    squares_ref[...] = first_ref[...] + by_user(terms, row_ref[...], squares_ref.shape[0])


def gram_call(kernel, pieces, others, users_group, name, held=()):
    size, cols = pieces[0].shape
    inputs = [*pieces, *others, *held]
    return pl.pallas_call(
        kernel,
        in_specs=[ANY] * len(pieces) + [VMEM] * (len(inputs) - len(pieces)),
        out_specs=[VMEM] * 2,
        out_shape=[
            jax.ShapeDtypeStruct((NP * NZ * size, cols), jnp.bfloat16),
            jax.ShapeDtypeStruct((users_group, 128), jnp.float32),
        ],
        scratch_shapes=[pltpu.SemaphoreType.DMA((len(pieces),))],
        input_output_aliases={len(inputs) - 1: 0} if held else {},
        compiler_params=params(20),
        cost_estimate=LITTLE,
        name=name,
    )(*inputs)


def transpose_kernel(place_ref, grad_ref, mine_ref, other_ref):
    core = place_ref[0]
    count, width, rows = mine_ref.shape
    size = rows // (NP * NZ)
    for n, start in enumerate(starts_of(place_ref, size)):
        turned = grad_ref[pl.ds(n * size, size), :].T
        inside = pl.ds(start, size)
        for k in range(count):
            first, second = (
                turned[(2 * k + i) * width : (2 * k + i + 1) * width] for i in range(2)
            )
            mine_ref[k, :, inside] = jnp.where(core == 0, first, second)
            other_ref[k, :, inside] = jnp.where(core == 0, second, first)


def transpose_call(place, grad, width):
    rows, cols = grad.shape
    count = cols // width // NC
    out = pl.BlockSpec((count // 2, width, rows), lambda i: (i, 0, 0))
    return pl.pallas_call(
        transpose_kernel,
        grid=(2,),
        in_specs=[SMEM, pl.BlockSpec((rows, cols // 2), lambda i: (0, i))],
        out_specs=[out, out],
        out_shape=[jax.ShapeDtypeStruct((count, width, rows), grad.dtype)] * 2,
        compiler_params=params(40, "arbitrary"),
        cost_estimate=LITTLE,
        name="transpose",
    )(place, grad)


def scaled_tile(
    clip_bound, place_ref, mine_ref, theirs_ref, squares_ref, more_ref, user_refs, hidden_refs,
    scaled_ref
):
    width, rows = mine_ref.shape[1:]
    count = squares_ref.shape[0] // 2
    ids = lax.broadcasted_iota(jnp.int32, (count, rows), 0)
    x_index, y_index = place_ref[1], place_ref[2]
    total = None
    for group, ref in enumerate((mine_ref, theirs_ref)):
        inside = pl.ds(group * count, count)
        squares = squares_ref[inside, 0:1] + more_ref[inside, 0:1]
        factor = clip_bound / jnp.maximum(jnp.sqrt(squares), clip_bound)
        chosen = jnp.where(ids == user_refs[group][...], factor, 0.0)
        row_factor = jnp.sum(chosen, axis=0, keepdims=True)
        for start in range(0, rows, 2 * TILE):
            parts = []
            for dx in range(NX):
                for dy in range(NY):
                    index = ((x_index + dx) % NX) * NY + (y_index + dy) % NY
                    block = ref[index, :, start : start + 2 * TILE].astype(jnp.float32)
                    parts.append(
                        (block * row_factor[:, start : start + 2 * TILE]).astype(jnp.bfloat16)
                    )
            scaled = jnp.concatenate(parts, axis=0)
            scaled_ref[:, pl.ds(group * rows + start, 2 * TILE)] = scaled
            part = jnp.dot(
                scaled,
                hidden_refs[group][pl.ds(start, 2 * TILE), :],
                preferred_element_type=jnp.float32,
            )
            total = part if total is None else total + part
    return total


def term_kernel(
    clip_bound, by_x, place_ref, mine_ref, theirs_ref, own_ref, sib_ref, squares_ref, more_ref,
    user_ref, user_sib_ref, after_ref, *refs
):
    outs, token_ref, scaled_ref = refs[:-2], refs[-2], refs[-1]
    token_ref[...] = jnp.zeros_like(token_ref)

    rows = own_ref.shape[0]

    def put(total):
        total = total.astype(jnp.bfloat16)
        size = mine_ref.shape[1]
        for dx in range(NX):
            for dy in range(NY):
                out, at = (outs[dx], dy) if by_x else (outs[2 * dy + dx // 2], dx % 2)
                out[pl.ds(at * size, size), :] = total[(dx * NY + dy) * size :][:size]

    @pl.when(pl.program_id(0) == 0)
    def _():
        put(
            scaled_tile(
                clip_bound, place_ref, mine_ref, theirs_ref, squares_ref, more_ref,
                (user_ref, user_sib_ref), (own_ref, sib_ref), scaled_ref,
            )
        )

    @pl.when(pl.program_id(0) > 0)
    def _():
        total = jnp.dot(scaled_ref[:, :rows], own_ref[...], preferred_element_type=jnp.float32)
        total += jnp.dot(scaled_ref[:, rows:], sib_ref[...], preferred_element_type=jnp.float32)
        put(total)


def term_call(
    by_x, place, mine, theirs, own, sib, squares, more, user_row, user_sib, clip_bound, start, cols,
    after
):
    count, width, rows = mine.shape
    whole = lambda a: pl.BlockSpec(a.shape, lambda n: (0,) * a.ndim)
    hidden = pl.BlockSpec((rows, TILE), lambda n: (0, n + start // TILE))
    pieces = NX if by_x else 2 * NY
    size = count * width // pieces
    small = [squares, more, user_row, user_sib]
    return pl.pallas_call(
        functools.partial(term_kernel, clip_bound, by_x),
        grid=(cols // TILE,),
        in_specs=[SMEM, whole(mine), whole(theirs), hidden, hidden] + [whole(a) for a in small] + [ANY],
        out_specs=[pl.BlockSpec((size, TILE), lambda n: (0, n))] * pieces + [whole(TOKEN)],
        out_shape=[jax.ShapeDtypeStruct((size, cols), jnp.bfloat16)] * pieces + [TOKEN],
        scratch_shapes=[pltpu.VMEM((count * width, 2 * rows), jnp.bfloat16)],
        compiler_params=params(40, "arbitrary"),
        cost_estimate=LITTLE,
        name="term_x" if by_x else "term_y",
    )(place, mine, theirs, own, sib, *small, after)


def add_x_kernel(*refs):
    parts, (_, keep_ref, send_ref) = refs[:-3], refs[-3:]
    width = keep_ref.shape[0]
    total = parts[0][...].astype(jnp.float32)
    for part in parts[1:]:
        total += part[...].astype(jnp.float32)
    keep_ref[...] = total[:width]
    send_ref[...] = total[width:].astype(jnp.bfloat16)


def add_y_kernel(first_low, first_high, second_low, second_high, after_ref, *outs):
    width = outs[0].shape[0]
    for half, (first, second) in enumerate(((first_low, second_low), (first_high, second_high))):
        total = first[...].astype(jnp.float32) + second[...].astype(jnp.float32)
        for k in range(2):
            out = outs[2 * half + k]
            out[...] = total[k * width : (k + 1) * width].astype(out.dtype)


def add_call(kernel, parts, width, sends, extra=()):
    cols = parts[0].shape[1]
    tile = lambda rows: pl.BlockSpec((rows, cols // 2), lambda n: (0, n))
    return pl.pallas_call(
        kernel,
        grid=(2,),
        in_specs=[tile(a.shape[0]) for a in parts] + [ANY] * len(extra),
        out_specs=[tile(width)] * (sends + 1),
        out_shape=[jax.ShapeDtypeStruct((width, cols), jnp.float32)]
        + [jax.ShapeDtypeStruct((width, cols), jnp.bfloat16)] * sends,
        compiler_params=params(40, "arbitrary"),
        cost_estimate=LITTLE,
        name="add",
    )(*parts, *extra)


def grads_kernel(place_ref, blocks_ref, same_ref, other_ref, gate_ref, up_ref, *refs):
    gate_grad_ref, up_grad_ref, token_ref, grad_ref, weight_ref = refs[-5:]

    @pl.when(pl.program_id(0) == 0)
    def _():
        size = grad_ref.shape[0] // (NP * NZ)
        for k, start in enumerate(starts_of(place_ref, size)):
            grad_ref[pl.ds(start, size), :] = blocks_ref[pl.ds(k * size, size), :]

    width = weight_ref.shape[0] // (NX * NY * NC)
    y_index = place_ref[2]
    for k in range(NX * NC):
        x, core = k // NC, k % NC
        for ref, y in ((same_ref, y_index), (other_ref, 1 - y_index)):
            start = pl.multiple_of(((x * NY + y) * NC + core) * width, width)
            weight_ref[pl.ds(start, width), :] = ref[pl.ds(k * width, width), :]
    token_ref[...] = jnp.zeros_like(token_ref)
    hidden_grad = jnp.dot(grad_ref[...], weight_ref[...], preferred_element_type=jnp.float32)
    gelu_value, gelu_slope = gelu_parts(gate_ref[...].astype(jnp.float32))
    gate_grad_ref[...] = (hidden_grad * up_ref[...].astype(jnp.float32) * gelu_slope).astype(
        jnp.bfloat16
    )
    up_grad_ref[...] = (hidden_grad * gelu_value).astype(jnp.bfloat16)


def grads_call(place, blocks, weights, gate, up, after, first, steps, held):
    rows, cols = gate.shape
    depth = blocks.shape[1]
    weight = pl.BlockSpec((depth // 2, TILE), lambda n: (0, n + first))
    tile = pl.BlockSpec((rows, TILE), lambda n: (0, n + first))
    return pl.pallas_call(
        grads_kernel,
        grid=(steps,),
        in_specs=[
            SMEM,
            pl.BlockSpec((rows, depth), lambda n: (0, 0)),
            weight,
            weight,
            tile,
            tile,
            ANY,
        ]
        + [ANY] * len(held),
        out_specs=[tile, tile, pl.BlockSpec(TOKEN.shape, lambda n: (0, 0))],
        out_shape=[jax.ShapeDtypeStruct((rows, cols), jnp.bfloat16)] * 2 + [TOKEN],
        scratch_shapes=[
            pltpu.VMEM((rows, depth), jnp.bfloat16), pltpu.VMEM((depth, TILE), jnp.bfloat16)
        ],
        input_output_aliases={7 + k: k for k in range(len(held))},
        compiler_params=params(52, "arbitrary"),
        cost_estimate=LITTLE,
        name="grads",
    )(place, blocks, *weights, gate, up, after, *held)


def update_kernel(scale, own_x, got_x, own_y, *refs):
    got_y, noise_ref, out_ref = refs[:-3], refs[-3], refs[-1]
    split = own_x.shape[1]
    total = own_x[...] + got_x[...].astype(jnp.float32)
    out_ref[:, :split] = scale * total + noise_ref[:, :split]
    total = own_y[...]
    for block in got_y:
        total += block[...].astype(jnp.float32)
    out_ref[:, split:] = scale * total + noise_ref[:, split:]


def update_call(scale, parts, noise, after):
    rows, cols = noise.shape
    spec = lambda a: pl.BlockSpec((rows // 3, a.shape[1]), lambda n: (n, 0))
    return pl.pallas_call(
        functools.partial(update_kernel, scale),
        grid=(3,),
        in_specs=[spec(a) for a in parts] + [spec(noise), ANY],
        out_specs=spec(noise),
        out_shape=jax.ShapeDtypeStruct(noise.shape, jnp.float32),
        compiler_params=params(24, "arbitrary"),
        cost_estimate=LITTLE,
        name="update",
    )(*parts, noise, after)


def local(gate_pre, up_pre, out_grad, down_weight, token_user, noise):
    users_group = USR_DEV * NP * NZ
    groups = NX * NY * NC
    clip_bound = 0.5 * math.sqrt(SLOTS * F * D)
    width = D // groups
    rows = gate_pre.shape[0]
    core = lax.axis_index("c")
    x_index = lax.axis_index("x")
    y_index = lax.axis_index("yh")

    weight = down_weight.T
    weight_other = lax.ppermute(weight, "yh", shift(NY, 1))
    pair = lax.axis_index("yl")
    ring = lax.axis_index("z")
    other = lax.ppermute(out_grad, "yl", shift(NP, 1))
    left = lax.ppermute(out_grad, "z", shift(NZ, 1))
    right = lax.ppermute(out_grad, "z", shift(NZ, -1))
    far = lax.ppermute(out_grad, "z", shift(NZ, 2))

    hidden = hidden_call(gate_pre, up_pre)
    other, left, right, far, hidden, weight_other = lax.optimization_barrier(
        (other, left, right, far, hidden, weight_other)
    )
    weights = [
        lax.all_gather(part, ("x", "c"), axis=0, tiled=True) for part in (weight, weight_other)
    ]
    other_left = lax.ppermute(other, "z", shift(NZ, 1))
    other_right = lax.ppermute(other, "z", shift(NZ, -1))
    other_far = lax.ppermute(far, "yl", shift(NP, 1))

    hidden_sib = lax.ppermute(hidden, "c", shift(NC, 1))
    user_row = token_user.reshape(1, rows)
    user_sib = lax.ppermute(user_row, "c", shift(NC, 1))
    place = [
        (at * NZ + (ring + step) % NZ) * out_grad.shape[0]
        for at in (pair, 1 - pair)
        for step in (0, 3, 1, 2)
    ]
    place = jnp.stack([core, x_index, y_index, *place]).astype(jnp.int32)
    pieces = [out_grad, left, right, far, other]
    gram_early, gram_late, user_order = hidden_gram_call(
        place, hidden, token_user, user_row, len(pieces) * out_grad.shape[0]
    )
    blocks, squares = gram_call(
        early_gram_kernel, pieces, [gram_early, user_order], users_group, "early_gram"
    )
    other_left, other_right, other_far, user_sib, squares = lax.optimization_barrier(
        (other_left, other_right, other_far, user_sib, squares)
    )
    blocks, squares = gram_call(
        late_gram_kernel,
        [other_left, other_right, other_far],
        [gram_late, user_order, squares],
        users_group,
        "late_gram",
        (blocks,),
    )
    mine, others = transpose_call(place, blocks, width)
    squares_sib = lax.ppermute(squares, "c", shift(NC, 1))
    squares_sib, others = lax.optimization_barrier((squares_sib, others))
    theirs = lax.ppermute(others, "c", shift(NC, 1))
    squares = jnp.concatenate([squares, squares_sib], axis=0)
    squares = squares + lax.ppermute(squares, "yl", shift(NP, 1))
    squares = squares + lax.ppermute(squares, "z", [(0, 1), (1, 0), (2, 3), (3, 2)])
    more = lax.ppermute(squares, "z", [(0, 3), (3, 0), (1, 2), (2, 1)])

    cols = hidden.shape[1]
    split = (cols // TILE + 1) // 2 * TILE
    term = lambda by_x, start, count, after: term_call(
        by_x, place, mine, theirs, hidden, hidden_sib, squares, more, user_row, user_sib,
        clip_bound, start, count, after,
    )
    *term_x, done = term(True, 0, split, place)
    got_x = {dx: lax.ppermute(term_x[dx], "x", shift(NX, dx)) for dx in (2, 1, 3)}
    *term_y, done = term(False, split, cols - split, done)
    got_y = [lax.ppermute(part, "yh", shift(NY, 1)) for part in term_y[2:]]

    steps = cols // TILE
    split_steps = (2 * steps) // 3 + 1
    *held, done = grads_call(place, blocks, weights, gate_pre, up_pre, done, 0, split_steps, ())

    keep_x, send_x = add_call(
        add_x_kernel, [term_x[0], *got_x.values()], width, 1, (done,)
    )
    last_x = lax.ppermute(send_x, "yh", shift(NY, 1))
    keep_y, *send_y = add_call(add_y_kernel, [*term_y[:2], *got_y], width, NX - 1, (done,))
    last_y = [lax.ppermute(send_y[dx - 1], "x", shift(NX, dx)) for dx in (2, 1, 3)]

    gate_grad, up_grad, done = grads_call(
        place, blocks, weights, gate_pre, up_pre, send_y[0], split_steps, steps - split_steps, held
    )
    scale = math.sqrt(F * D) / (users_group * groups * clip_bound)
    weight_update = update_call(
        scale, [keep_x, last_x, keep_y, *last_y], noise.T, done
    ).T
    return (gate_grad, up_grad, weight_update)


def solution(mesh):
    fine = Mesh(mesh.devices.reshape(NX, NY, NC, NP, NZ), ("x", "yh", "c", "yl", "z"))
    fsdp = ("x", "yh", "c")
    user = ("yl", "z")
    return jax.shard_map(
        local,
        mesh=fine,
        in_specs=(
            P(fsdp, user),
            P(fsdp, user),
            P(fsdp + user, None),
            P(user, fsdp),
            P(fsdp, None),
            P(user, fsdp),
        ),
        out_specs=(P(fsdp, user), P(fsdp, user), P(user, fsdp)),
        check_vma=False,
    )
```
